512 devices in a mesh: ctx: 128 (over y, z, core), head: 4 (over x).
Axes of the slice: x: 4, y: 8, z: 8, core: 2. Of those that a mesh axis runs over, the one named last changes fastest.
Arguments:
- queries: bfloat16 [3, 8, 8192], P(None, None, 'head'), may hold values from -8 to 8
- k_cache: bfloat16 [8, 32768, 1024], P(None, 'ctx', 'head'), may hold values from -6 to 6
- v_cache: bfloat16 [8, 32768, 1024], P(None, 'ctx', 'head'), may hold values from -6 to 6
- new_keys: bfloat16 [3, 8, 1024], P(None, None, 'head'), may hold values from -6 to 6
- new_values: bfloat16 [3, 8, 1024], P(None, None, 'head'), may hold values from -6 to 6
- fill: int32 [8, 128], P(None, 'ctx'), may hold values from 2 to 253, as said below
- owner: int32 [3, 8], replicated, may hold values from 0 to 127
- out_weight: bfloat16 [8192, 8192], P('head', 'ctx'), may hold values from -0.25 to 0.25
Outputs:
- keys_out: bfloat16 [8, 32768, 1024], P(None, 'ctx', 'head')
- values_out: bfloat16 [8, 32768, 1024], P(None, 'ctx', 'head')
- mixed: bfloat16 [3, 8, 8192], P(None, None, ('ctx', 'head'))
The draws below stay inside these ranges and needn't reach their ends.
Inputs may be any that keep to these rules, and one draw needn't show every extreme that they name: Rows 0 to fill - 1 of each shard hold the sequence's earlier positions; some entry equals 253.
All inputs are finite; a program needn't handle non-finite values.
Results may differ from the reference program's by a relative error of at most 0.0051.
Values may be sent and summed in bfloat16 or wider, within the bound.
No kernel may reach another device: no remote copies, remote signals or barrier semaphores. Data moves between devices by JAX's collectives and lax.ppermute only.
A program may use at most 128 MiB of HBM per device.

```python
import jax
import jax.numpy as jnp
from jax import lax

D = 8192
HQ = 64
KVH = 8
HD = 128
BATCH = 8
ROWS = 256
STEPS = 3
CONTEXT = 32768
N_CTX = 128


def draw_queries(key, part):
    key = jax.random.fold_in(key, 11)
    base = jnp.clip(2.0 * jax.random.normal(key, (STEPS, BATCH, HQ * HD), jnp.float32), -8.0, 8.0)
    return base.astype(jnp.bfloat16)


def draw_k_cache(key, part):
    key = jax.random.fold_in(key, 12)
    base = jnp.clip(jax.random.normal(key, (BATCH, CONTEXT, KVH * HD), jnp.float32), -6.0, 6.0)
    return base.astype(jnp.bfloat16)


def draw_fill(key, part):
    key = jax.random.fold_in(key, 13)
    shards = CONTEXT // ROWS
    most = ROWS - STEPS
    values = jax.random.randint(key, (BATCH, shards), 2, most + 1)
    which_row = jax.random.randint(jax.random.fold_in(key, 1), (), 0, BATCH)
    which_shard = jax.random.randint(jax.random.fold_in(key, 2), (), 0, shards)
    row_ids = jax.lax.broadcasted_iota(jnp.int32, (BATCH, shards), 0)
    shard_ids = jax.lax.broadcasted_iota(jnp.int32, (BATCH, shards), 1)
    chosen = (row_ids == which_row) & (shard_ids == which_shard)
    return jnp.where(chosen, most, values).astype(jnp.int32)


def place_ends(values, stream_key, low, high):
    dims = values.shape
    spot = [jax.random.randint(jax.random.fold_in(stream_key, axis), (), 0, dims[axis]) for axis in range(len(dims))]
    values = values.at[tuple(spot)].set(low)
    longest = dims.index(max(dims))
    spot[longest] = (spot[longest] + 1) % dims[longest]
    return values.at[tuple(spot)].set(high)


def strengthened(entries, key, source, target, blocks, factor):
    owner, partner = [(jnp.arange(entries.shape[position]) // (entries.shape[position] // blocks)).reshape([-1 if axis == position else 1 for axis in range(entries.ndim)]) for position in (source, target)]
    chosen = jax.random.permutation(key, blocks)[partner]
    strong = (owner == chosen) | (owner == (partner + blocks // 2) % blocks)
    return jnp.where(strong, factor * entries, entries)


def shard_levels(rng, extent, cuts, smallest, high):
    loudness = 1.0
    for position, blocks in cuts:
        steps = jax.random.uniform(jax.random.fold_in(jax.random.fold_in(rng, 6), position), (blocks,), jnp.float32, smallest / len(cuts), high / len(cuts))
        loudness = loudness * jnp.repeat(jnp.exp(steps), extent[position] // blocks).reshape((-1,) + (1,) * (len(extent) - 1 - position))
    return loudness


def gaussian(own_key, extent, scale, limit, pieces=(), kind=jnp.bfloat16):
    level = shard_levels(own_key, extent, pieces, -0.22, 0.18) if pieces else 1.0
    values = jax.random.normal(own_key, extent, jnp.float32) * scale * level
    return jnp.minimum(jnp.maximum(values, -limit), limit).astype(kind)


def noise_with(stream_key, extent, width, bound, pieces, heavy, kind=jnp.bfloat16):
    values = width * jax.random.normal(stream_key, extent, jnp.float32)
    if pieces:
        values = values * shard_levels(stream_key, extent, pieces, -0.22, 0.18)
    return jnp.clip(strengthened(values, jax.random.fold_in(stream_key, 3), *heavy), -bound, bound).astype(kind)


def setup_inputs(seed: int = 0) -> dict:
    keys = jax.random.split(jax.random.key(seed), 9)
    queries = draw_queries(jax.random.fold_in(keys[8], 71), 0)
    k_cache = draw_k_cache(jax.random.fold_in(keys[8], 71), 0)
    v_cache = gaussian(keys[2], (BATCH, CONTEXT, KVH * HD), 1.0, 6.0, ((1, 128), (2, 4)))
    new_keys = gaussian(keys[3], (STEPS, BATCH, KVH * HD), 1.0, 6.0, ((2, 4),))
    new_values = gaussian(keys[4], (STEPS, BATCH, KVH * HD), 1.0, 6.0, ((2, 4),))
    fill = draw_fill(jax.random.fold_in(keys[8], 71), 0)
    owner = place_ends(jax.random.randint(keys[6], (STEPS, BATCH), 0, N_CTX), jax.random.fold_in(keys[6], 1), 0, N_CTX - 1).astype(jnp.int32)
    out_weight = noise_with(keys[7], (D, D), D ** -0.5, 0.25, ((0, 4), (1, 128)), (0, 1, 128, 5.5))
    return {"queries": queries, "k_cache": k_cache, "v_cache": v_cache, "new_keys": new_keys, "new_values": new_values, "fill": fill, "owner": owner, "out_weight": out_weight}


def attend(packed):
    query_rows, key_rows, value_rows, live_len = packed
    groups = HQ // KVH
    shards = key_rows.shape[0] // ROWS
    query_heads = query_rows.reshape(STEPS, KVH, groups, HD).astype(jnp.float32)
    key_heads = key_rows.reshape(shards, ROWS, KVH, HD).astype(jnp.float32)
    value_heads = value_rows.reshape(shards, ROWS, KVH, HD).astype(jnp.float32)
    scores = jnp.einsum('sgqd,crgd->sgqcr', query_heads, key_heads) * (1.0 / HD ** 0.5)
    slots = jnp.arange(ROWS, dtype=jnp.int32)
    live = (slots[None, None, :] < live_len[:, :, None])[:, None, None, :, :]
    masked = jnp.where(live, scores, -1e30)
    peak = jnp.max(masked, axis=-1)
    weights = jnp.where(live, jnp.exp(masked - peak[..., None]), 0.0)
    total = jnp.sum(weights, axis=-1)
    rounded = weights.astype(jnp.bfloat16)
    rounded = lax.optimization_barrier(rounded).astype(jnp.float32)
    part = jnp.einsum('sgqcr,crgd->sgqcd', rounded, value_heads)
    largest = jnp.max(peak, axis=-1)
    factor = jnp.exp(peak - largest[..., None])
    numer = jnp.sum(part * factor[..., None], axis=-2)
    denom = jnp.sum(total * factor, axis=-1)
    return (numer / denom[..., None]).astype(jnp.bfloat16).reshape(STEPS, HQ * HD)


def reference(queries, k_cache, v_cache, new_keys, new_values, fill, owner, out_weight):
    shards = fill.shape[1]
    batch_ids = jnp.arange(BATCH, dtype=jnp.int32)
    onehot = (owner[:, :, None] == jnp.arange(shards, dtype=jnp.int32)[None, None, :]).astype(jnp.int32)
    counted = jnp.cumsum(onehot, axis=0).astype(jnp.int32)
    keys_out, values_out = k_cache, v_cache
    for step in range(STEPS):
        target = owner[step]
        base_fill = jnp.take_along_axis(fill, target[:, None], axis=1)[:, 0]
        seen = jnp.take_along_axis(counted[step], target[:, None], axis=1)[:, 0]
        row_index = (target * ROWS + base_fill + seen - 1).astype(jnp.int32)
        keys_out = keys_out.at[batch_ids, row_index].set(new_keys[step])
        values_out = values_out.at[batch_ids, row_index].set(new_values[step])
    lengths = (fill[None, :, :] + counted).astype(jnp.int32)
    attention = lax.map(attend, (jnp.transpose(queries, (1, 0, 2)), keys_out, values_out, jnp.transpose(lengths, (1, 0, 2))))
    attention = jnp.transpose(attention, (1, 0, 2)).reshape(STEPS * BATCH, HQ * HD)
    mixed = jnp.dot(attention, out_weight, preferred_element_type=jnp.float32).astype(jnp.bfloat16)
    return keys_out, values_out, mixed.reshape(STEPS, BATCH, D)
```

```python
import functools

import jax
import jax.numpy as jnp
from jax import lax
from jax.experimental import pallas as pl
from jax.experimental.pallas import tpu as pltpu
from jax.sharding import Mesh
from jax.sharding import PartitionSpec as P

HD = 128
F32 = jnp.float32
BF16 = jnp.bfloat16
ATTEND_VMEM = 63_000_000
CTX = ("y", "z", "core")


def three_way(x):
    first = x.astype(BF16).astype(F32)
    rest = x - first
    second = rest.astype(BF16).astype(F32)
    return first, second, rest - second


def stat_rows(peak, total):
    shape = (8, peak.shape[1])
    row = lax.broadcasted_iota(jnp.int32, shape, 0)
    out = jnp.zeros(shape, F32)
    for i, part in enumerate(three_way(peak) + three_way(total)):
        out = jnp.where(row == i, jnp.broadcast_to(part, shape), out)
    return out


def attend_kernel(
    fill_ref, owner_ref, q_ref, k_hbm, v_hbm, nk_ref, nv_ref,
    ko_hbm, vo_hbm, out_ref, q_vmem, nk_vmem, nv_vmem, k_ref, v_ref, in_sem, k_sem, v_sem, ko_sem, vo_sem,
):
    steps, batch, width = q_ref.shape
    small = [
        pltpu.make_async_copy(src, dst, in_sem.at[i])
        for i, (src, dst) in enumerate(((q_ref, q_vmem), (nk_ref, nk_vmem), (nv_ref, nv_vmem)))
    ]
    for copy in small:
        copy.start()
    rows = k_ref.shape[1]
    heads = width // HD
    per_kv = heads // 2
    n = per_kv * steps * batch
    loads = []
    for b in range(batch):
        pair = (
            pltpu.make_async_copy(k_hbm.at[b], k_ref.at[b], k_sem.at[b]),
            pltpu.make_async_copy(v_hbm.at[b], v_ref.at[b], v_sem.at[b]),
        )
        pair[0].start()
        pair[1].start()
        loads.append(pair)

    me = lax.axis_index(CTX)
    lane = lax.broadcasted_iota(jnp.int32, (batch, rows), 1)
    sub = lax.broadcasted_iota(jnp.int32, (batch, rows), 0)
    live_steps = []
    slots = []
    seen = [jnp.int32(0)] * batch
    for s in range(steps):
        length = jnp.zeros((batch, rows), jnp.int32)
        for b in range(batch):
            mine = owner_ref[s, b] == me
            seen[b] = seen[b] + mine.astype(jnp.int32)
            end = fill_ref[0, b] + seen[b]
            slots.append((s, b, mine, end - 1))
            length = jnp.where(sub == b, end, length)
        live_steps.append(lane < length)
    live = jnp.concatenate(live_steps * per_kv, axis=0)

    for copy in small:
        copy.wait()
    q = q_vmem[...].astype(F32).reshape(steps * batch, width)
    q_groups = [
        jnp.concatenate([q[:, (g * per_kv + h) * HD : (g * per_kv + h + 1) * HD] for h in range(per_kv)], axis=0)
        for g in range(2)
    ]

    stores = []
    for b in range(batch):
        loads[b][0].wait()
        loads[b][1].wait()
        for s, sb, mine, slot in slots:
            if sb != b:
                continue

            @pl.when(mine)
            def _(s=s, slot=slot):
                base = pl.multiple_of((slot // 16) * 16, 16)
                at = lax.broadcasted_iota(jnp.int32, (16, 2 * HD), 0) == slot - base
                for ref, new in ((k_ref, nk_vmem), (v_ref, nv_vmem)):
                    old = ref[b, pl.ds(base, 16), :].astype(F32)
                    row = new[s, b : b + 1, :].astype(F32)
                    ref[b, pl.ds(base, 16), :] = jnp.where(at, jnp.broadcast_to(row, at.shape), old).astype(BF16)

        pair = (
            pltpu.make_async_copy(k_ref.at[b], ko_hbm.at[b], ko_sem.at[b]),
            pltpu.make_async_copy(v_ref.at[b], vo_hbm.at[b], vo_sem.at[b]),
        )
        pair[0].start()
        pair[1].start()
        stores.append(pair)

    which = lax.broadcasted_iota(jnp.int32, (n, HD), 0) % batch
    which_rows = lax.broadcasted_iota(jnp.int32, (n, rows), 0) % batch
    parts, stats = [], []
    for g in range(2):
        cols = slice(g * HD, (g + 1) * HD)
        scores = jnp.zeros((n, rows), F32)
        for p in range(0, batch, 2):
            lhs = jnp.concatenate(
                [jnp.where(which == p, q_groups[g], 0.0), jnp.where(which == p + 1, q_groups[g], 0.0)], axis=1
            ).astype(BF16)
            rhs = jnp.concatenate([k_ref[p, :, cols], k_ref[p + 1, :, cols]], axis=1)
            scores = scores + lax.dot_general(lhs, rhs, (((1,), (1,)), ((), ())), preferred_element_type=F32)
        masked = jnp.where(live, scores * (1.0 / HD**0.5), -1e30)
        peak = jnp.max(masked, axis=1, keepdims=True)
        weights = jnp.where(live, jnp.exp(masked - peak), 0.0)
        total = jnp.sum(weights, axis=1, keepdims=True)
        part = jnp.zeros((n, HD), F32)
        for b in range(batch):
            lhs = jnp.where(which_rows == b, weights, 0.0).astype(BF16)
            part = part + jnp.dot(lhs, v_ref[b, :, cols], preferred_element_type=F32)
        parts.append(part)
        col = lax.broadcasted_iota(jnp.int32, (n, HD), 1)
        stats.append(
            jnp.where(col == 0, jnp.broadcast_to(peak, (n, HD)), jnp.where(col == 1, jnp.broadcast_to(total, (n, HD)), 0.0))
        )
    part_t = jnp.concatenate(parts, axis=0).T
    stat_t = jnp.concatenate(stats, axis=0).T
    stat = stat_rows(stat_t[0:1], stat_t[1:2])
    dests = out_ref.shape[0]
    each = HD // dests
    for d in range(dests):
        out_ref[d] = jnp.concatenate([part_t[d * each : (d + 1) * each], stat], axis=0).astype(BF16)
    for pair in stores:
        pair[0].wait()
        pair[1].wait()


def combined(in_ref, each):
    x = in_ref[...].astype(F32)
    stat = x[:, each:]
    row = lax.broadcasted_iota(jnp.int32, stat.shape, 1)
    peak = jnp.sum(jnp.where(row < 3, stat, 0.0), axis=1, keepdims=True)
    total = jnp.sum(jnp.where((row >= 3) & (row < 6), stat, 0.0), axis=1, keepdims=True)
    top = jnp.max(peak, axis=0, keepdims=True)
    factor = jnp.exp(peak - top)
    return jnp.sum(x[:, :each] * factor, axis=0), top[0], jnp.sum(total * factor, axis=0)


def partial_kernel(in_ref, out_ref, *, each):
    part, top, total = combined(in_ref, each)
    block = jnp.concatenate([part, stat_rows(top, total)], axis=0).astype(BF16)
    for d in range(out_ref.shape[0]):
        out_ref[d] = block


def final_kernel(in_ref, out_ref, *, each):
    part, _, total = combined(in_ref, each)
    block = (part / total).astype(BF16)
    for d in range(out_ref.shape[0]):
        out_ref[d] = block


def project_kernel(in_ref, w_ref, out_ref):
    sources, each, n = in_ref.shape
    rows, cols = out_ref.shape[1], w_ref.shape[0]
    attention = in_ref[...].astype(F32).reshape(sources * each, n).T
    wide = jnp.concatenate([attention[h * rows : (h + 1) * rows] for h in range(n // rows)], axis=1)
    mixed = lax.dot_general(wide.astype(BF16), w_ref[...], (((1,), (1,)), ((), ())), preferred_element_type=F32)
    block = jnp.concatenate([mixed, jnp.zeros((rows, out_ref.shape[2] - cols), F32)], axis=1)
    for d in range(out_ref.shape[0]):
        out_ref[d] = block


def finish_kernel(in_ref, out_ref):
    steps, batch, cols = out_ref.shape
    x = in_ref[...]
    total = x[0]
    for d in range(1, x.shape[0]):
        total = total + x[d]
    me = lax.axis_index("head")
    mine = total[:, :cols]
    for d in range(1, x.shape[0]):
        mine = jnp.where(me == d, total[:, d * cols : (d + 1) * cols], mine)
    out_ref[...] = mine.reshape(steps, batch, cols).astype(BF16)


VMEM = pl.BlockSpec(memory_space=pltpu.VMEM)
SMEM = pl.BlockSpec(memory_space=pltpu.SMEM)
HBM = pl.BlockSpec(memory_space=pltpu.HBM)


def on_device(n_y, n_zc, n_head, queries, k_cache, v_cache, new_keys, new_values, fill, owner, out_weight):
    steps, batch, width = queries.shape
    rows = k_cache.shape[1]
    n = steps * batch * (width // HD)
    each = HD // n_zc
    struct = jax.ShapeDtypeStruct
    params = lambda mib: pltpu.CompilerParams(vmem_limit_bytes=mib * 2**20)
    keys_out, values_out, sent = pl.pallas_call(
        attend_kernel,
        out_shape=(
            struct(k_cache.shape, BF16),
            struct(v_cache.shape, BF16),
            struct((n_zc, each + 8, n), BF16),
        ),
        in_specs=[SMEM, SMEM, HBM, HBM, HBM, HBM, HBM],
        out_specs=(HBM, HBM, VMEM),
        scratch_shapes=[
            pltpu.VMEM(queries.shape, BF16),
            pltpu.VMEM(new_keys.shape, BF16),
            pltpu.VMEM(new_values.shape, BF16),
            pltpu.VMEM(k_cache.shape, BF16),
            pltpu.VMEM(v_cache.shape, BF16),
        ]
        + [pltpu.SemaphoreType.DMA((3,))]
        + [pltpu.SemaphoreType.DMA((batch,))] * 4,
        compiler_params=pltpu.CompilerParams(vmem_limit_bytes=ATTEND_VMEM),
        name="attend",
    )(fill.T, owner, queries, k_cache, v_cache, new_keys, new_values)
    got = lax.all_to_all(sent, ("z", "core"), 0, 0)
    sent = pl.pallas_call(
        functools.partial(partial_kernel, each=each),
        out_shape=struct((n_y, each + 8, n), BF16),
        in_specs=[VMEM],
        out_specs=VMEM,
        compiler_params=params(8),
        name="combine_zc",
    )(got)
    got = lax.all_to_all(sent, "y", 0, 0)
    sent = pl.pallas_call(
        functools.partial(final_kernel, each=each),
        out_shape=struct((n_zc, each, n), BF16),
        in_specs=[VMEM],
        out_specs=VMEM,
        compiler_params=params(8),
        name="combine_y",
    )(got)
    got = lax.all_to_all(sent, ("z", "core"), 0, 0)
    sent = pl.pallas_call(
        project_kernel,
        out_shape=struct((n_head, steps * batch, 128), F32),
        in_specs=[VMEM, VMEM],
        out_specs=VMEM,
        compiler_params=params(8),
        name="project",
    )(got, out_weight.T)
    got = lax.all_to_all(sent, "head", 0, 0)
    mixed = pl.pallas_call(
        finish_kernel,
        out_shape=struct((steps, batch, out_weight.shape[1] // n_head), BF16),
        in_specs=[VMEM],
        out_specs=VMEM,
        compiler_params=params(8),
        name="finish",
    )(got)
    return keys_out, values_out, mixed


def solution(mesh):
    n_ctx, n_head = mesh.devices.shape
    n_y, n_z = 8, n_ctx // 16
    split = Mesh(mesh.devices.reshape(n_y, n_z, 2, n_head), CTX + ("head",))
    in_specs = (
        P(None, None, "head"),
        P(None, CTX, "head"),
        P(None, CTX, "head"),
        P(None, None, "head"),
        P(None, None, "head"),
        P(None, CTX),
        P(),
        P("head", CTX),
    )
    out_specs = (P(None, CTX, "head"), P(None, CTX, "head"), P(None, None, CTX + ("head",)))
    return jax.shard_map(
        functools.partial(on_device, n_y, n_z * 2, n_head),
        mesh=split, in_specs=in_specs, out_specs=out_specs, check_vma=False,
    )
```

```python
import functools

import jax
import jax.numpy as jnp
from jax import lax
from jax.experimental import pallas as pl
from jax.experimental.pallas import tpu as pltpu
from jax.sharding import Mesh
from jax.sharding import PartitionSpec as P

HD = 128
F32 = jnp.float32
BF16 = jnp.bfloat16
ATTEND_VMEM = 63_000_000
CHUNKS = 2
CTX = ("y", "z", "core")


def three_way(x):
    first = x.astype(BF16).astype(F32)
    rest = x - first
    second = rest.astype(BF16).astype(F32)
    return first, second, rest - second


def attend_kernel(
    fill_hbm, owner_hbm, q_hbm, k_hbm, v_hbm, nk_hbm, nv_hbm,
    ko_hbm, vo_hbm, out_ref,
    fill_ref, owner_ref, q_ref, nk_ref, nv_ref, k_ref, v_ref, q_rows, rows_out, in_sem, load_sem, store_sem,
):
    steps, batch, width = q_ref.shape
    slots = k_ref.shape[1]
    heads = width // HD
    per_kv = heads // 2
    n = steps * heads
    size = batch // CHUNKS
    small = [
        pltpu.make_async_copy(src, dst, in_sem.at[i])
        for i, (src, dst) in enumerate(
            ((q_hbm, q_ref), (fill_hbm, fill_ref), (owner_hbm, owner_ref), (nk_hbm, nk_ref), (nv_hbm, nv_ref))
        )
    ]
    loads, stores = [], []
    for c in range(CHUNKS):
        part = pl.ds(c * size, size)
        for i, (hbm, vmem, out) in enumerate(((k_hbm, k_ref, ko_hbm), (v_hbm, v_ref, vo_hbm))):
            loads.append(pltpu.make_async_copy(hbm.at[part], vmem.at[part], load_sem.at[i, c]))
            stores.append(pltpu.make_async_copy(vmem.at[part], out.at[part], store_sem.at[i, c]))
    for copy in small + loads:
        copy.start()

    me = lax.axis_index(CTX)
    small[0].wait()
    q = q_ref[...].astype(F32)
    for s in range(steps):
        for h in range(heads):
            q_rows[:, s * heads + h, :] = q[s, :, h * HD : (h + 1) * HD]
    for copy in small[1:]:
        copy.wait()

    row = lax.broadcasted_iota(jnp.int32, (n, slots), 0)
    slot_id = lax.broadcasted_iota(jnp.int32, (n, slots), 1)
    lane = lax.broadcasted_iota(jnp.int32, (heads, HD), 1)
    peaks = jnp.zeros((heads, HD), F32)
    totals = jnp.zeros((heads, HD), F32)
    for c in range(CHUNKS):
        loads[2 * c].wait()
        loads[2 * c + 1].wait()
        ends = {}
        for b in range(c * size, (c + 1) * size):
            seen = jnp.int32(0)
            for s in range(steps):
                mine = owner_ref[s, b] == me
                seen = seen + mine.astype(jnp.int32)
                end = fill_ref[0, b] + seen
                ends[s, b] = end

                @pl.when(mine)
                def _(s=s, b=b, slot=end - 1):
                    base = pl.multiple_of((slot // 16) * 16, 16)
                    at = lax.broadcasted_iota(jnp.int32, (16, 2 * HD), 0) == slot - base
                    for ref, new in ((k_ref, nk_ref), (v_ref, nv_ref)):
                        old = ref[b, pl.ds(base, 16), :].astype(F32)
                        fresh = new[s, b : b + 1, :].astype(F32)
                        ref[b, pl.ds(base, 16), :] = jnp.where(at, jnp.broadcast_to(fresh, at.shape), old).astype(BF16)

        stores[2 * c].start()
        stores[2 * c + 1].start()
        for b in range(c * size, (c + 1) * size):
            length = jnp.where(row < heads, ends[0, b], ends[steps - 1, b])
            for s in range(1, steps - 1):
                length = jnp.where((row >= s * heads) & (row < (s + 1) * heads), ends[s, b], length)
            live = slot_id < length
            q_b = q_rows[b]
            first = (lax.broadcasted_iota(jnp.int32, (n, HD), 0) // per_kv) % 2 == 0
            lhs = jnp.concatenate([jnp.where(first, q_b, 0.0), jnp.where(first, 0.0, q_b)], axis=1).astype(BF16)
            scores = lax.dot_general(lhs, k_ref[b], (((1,), (1,)), ((), ())), preferred_element_type=F32)
            masked = jnp.where(live, scores * (1.0 / HD**0.5), -1e30)
            peak = jnp.max(masked, axis=1, keepdims=True)
            weights = jnp.where(live, jnp.exp(masked - peak), 0.0)
            total = jnp.sum(weights, axis=1, keepdims=True)
            both = jnp.dot(weights.astype(BF16), v_ref[b], preferred_element_type=F32)
            part = jnp.where(first, both[:, :HD], both[:, HD:])
            for s in range(steps):
                own = slice(s * heads, (s + 1) * heads)
                at = s * batch + b
                rows_out[:, at, :] = part[own]
                peaks = jnp.where(lane == at, peak[own], peaks)
                totals = jnp.where(lane == at, total[own], totals)
    used = steps * batch
    for i, piece in enumerate(three_way(peaks) + three_way(totals)):
        rows_out[:, used + i, :] = piece
    for i in range(6, 8):
        rows_out[:, used + i, :] = jnp.zeros((heads, HD), F32)
    for h in range(heads):
        out_ref[h] = rows_out[h].astype(BF16)
    for copy in stores:
        copy.wait()


def combined(in_ref):
    x = in_ref[...].astype(F32)
    used = x.shape[1] - 8
    stat = x[:, used:]
    row = lax.broadcasted_iota(jnp.int32, stat.shape, 1)
    peak = jnp.sum(jnp.where(row < 3, stat, 0.0), axis=1, keepdims=True)
    total = jnp.sum(jnp.where((row >= 3) & (row < 6), stat, 0.0), axis=1, keepdims=True)
    top = jnp.max(peak, axis=0, keepdims=True)
    factor = jnp.exp(peak - top)
    return x[:, :used], factor, top[0], jnp.sum(total * factor, axis=0)


def weighted(parts, factor):
    sources, rows, lanes = parts.shape
    shape = (1, rows, lanes)
    diagonal = lax.broadcasted_iota(jnp.int32, shape, 1) == lax.broadcasted_iota(jnp.int32, shape, 2)
    column = jnp.sum(jnp.where(diagonal, factor, 0.0), axis=2, keepdims=True)
    return jnp.sum(parts * column, axis=0)


def partial_kernel(in_ref, out_ref):
    parts, factor, top, total = combined(in_ref)
    row = lax.broadcasted_iota(jnp.int32, (8, HD), 0)
    stat = jnp.zeros((8, HD), F32)
    for i, piece in enumerate(three_way(top) + three_way(total)):
        stat = jnp.where(row == i, jnp.broadcast_to(piece, stat.shape), stat)
    block = jnp.concatenate([weighted(parts, factor), stat], axis=0).astype(BF16)
    for d in range(out_ref.shape[0]):
        out_ref[d] = block


def final_kernel(in_ref, out_ref):
    parts, factor, _, total = combined(in_ref)
    used = lax.broadcasted_iota(jnp.int32, total.shape, 1) < parts.shape[1]
    block = weighted(parts, factor / jnp.where(used, total, 1.0)[None]).astype(BF16)
    for d in range(out_ref.shape[0]):
        out_ref[d] = block


def project_kernel(in_ref, w_ref, out_ref):
    rows, cols = out_ref.shape[1], w_ref.shape[0]
    wide = jnp.concatenate([in_ref[h] for h in range(in_ref.shape[0])], axis=1)
    mixed = lax.dot_general(wide, w_ref[...], (((1,), (1,)), ((), ())), preferred_element_type=F32)
    block = jnp.concatenate([mixed, jnp.zeros((rows, out_ref.shape[2] - cols), F32)], axis=1)
    for d in range(out_ref.shape[0]):
        out_ref[d] = block


def finish_kernel(in_ref, out_ref):
    steps, batch, cols = out_ref.shape
    x = in_ref[...]
    total = x[0]
    for d in range(1, x.shape[0]):
        total = total + x[d]
    me = lax.axis_index("head")
    mine = total[:, :cols]
    for d in range(1, x.shape[0]):
        mine = jnp.where(me == d, total[:, d * cols : (d + 1) * cols], mine)
    out_ref[...] = mine.reshape(steps, batch, cols).astype(BF16)


VMEM = pl.BlockSpec(memory_space=pltpu.VMEM)
SMEM = pl.BlockSpec(memory_space=pltpu.SMEM)
HBM = pl.BlockSpec(memory_space=pltpu.HBM)


def on_device(n_y, n_zc, n_head, queries, k_cache, v_cache, new_keys, new_values, fill, owner, out_weight):
    steps, batch, width = queries.shape
    heads = width // HD
    used = steps * batch
    struct = jax.ShapeDtypeStruct
    params = lambda mib: pltpu.CompilerParams(vmem_limit_bytes=mib * 2**20)
    keys_out, values_out, sent = pl.pallas_call(
        attend_kernel,
        out_shape=(
            struct(k_cache.shape, BF16),
            struct(v_cache.shape, BF16),
            struct((n_zc, used + 8, HD), BF16),
        ),
        in_specs=[HBM] * 7,
        out_specs=(HBM, HBM, VMEM),
        scratch_shapes=[
            pltpu.SMEM((1, batch), jnp.int32),
            pltpu.SMEM(owner.shape, jnp.int32),
            pltpu.VMEM(queries.shape, BF16),
            pltpu.VMEM(new_keys.shape, BF16),
            pltpu.VMEM(new_values.shape, BF16),
            pltpu.VMEM(k_cache.shape, BF16),
            pltpu.VMEM(v_cache.shape, BF16),
            pltpu.VMEM((batch, steps * heads, HD), F32),
            pltpu.VMEM((heads, used + 8, HD), F32),
            pltpu.SemaphoreType.DMA((5,)),
            pltpu.SemaphoreType.DMA((2, CHUNKS)),
            pltpu.SemaphoreType.DMA((2, CHUNKS)),
        ],
        compiler_params=pltpu.CompilerParams(vmem_limit_bytes=ATTEND_VMEM),
        name="attend",
    )(fill.T, owner, queries, k_cache, v_cache, new_keys, new_values)
    got = lax.all_to_all(sent, ("z", "core"), 0, 0)
    sent = pl.pallas_call(
        partial_kernel,
        out_shape=struct((n_y, used + 8, HD), BF16),
        in_specs=[VMEM],
        out_specs=VMEM,
        compiler_params=params(8),
        name="combine_zc",
    )(got)
    got = lax.all_to_all(sent, "y", 0, 0)
    sent = pl.pallas_call(
        final_kernel,
        out_shape=struct((n_zc, used, HD), BF16),
        in_specs=[VMEM],
        out_specs=VMEM,
        compiler_params=params(8),
        name="combine_y",
    )(got)
    got = lax.all_to_all(sent, ("z", "core"), 0, 0)
    sent = pl.pallas_call(
        project_kernel,
        out_shape=struct((n_head, steps * batch, 128), F32),
        in_specs=[VMEM, VMEM],
        out_specs=VMEM,
        compiler_params=params(8),
        name="project",
    )(got, out_weight.T)
    got = lax.all_to_all(sent, "head", 0, 0)
    mixed = pl.pallas_call(
        finish_kernel,
        out_shape=struct((steps, batch, out_weight.shape[1] // n_head), BF16),
        in_specs=[VMEM],
        out_specs=VMEM,
        compiler_params=params(8),
        name="finish",
    )(got)
    return keys_out, values_out, mixed


def solution(mesh):
    n_ctx, n_head = mesh.devices.shape
    n_y, n_z = 8, n_ctx // 16
    split = Mesh(mesh.devices.reshape(n_y, n_z, 2, n_head), CTX + ("head",))
    in_specs = (
        P(None, None, "head"),
        P(None, CTX, "head"),
        P(None, CTX, "head"),
        P(None, None, "head"),
        P(None, None, "head"),
        P(None, CTX),
        P(),
        P("head", CTX),
    )
    out_specs = (P(None, CTX, "head"), P(None, CTX, "head"), P(None, None, CTX + ("head",)))
    return jax.shard_map(
        functools.partial(on_device, n_y, n_z * 2, n_head),
        mesh=split, in_specs=in_specs, out_specs=out_specs, check_vma=False,
    )
```

```python
import functools

import jax
import jax.numpy as jnp
from jax import lax
from jax.experimental import pallas as pl
from jax.experimental.pallas import tpu as pltpu
from jax.sharding import Mesh
from jax.sharding import PartitionSpec as P

HD = 128
F32 = jnp.float32
BF16 = jnp.bfloat16
ATTEND_VMEM = 63_000_000
CHUNKS = 2
CTX = ("y2", "y1", "y0", "z2", "z1", "z0", "core")
HEAD = ("x1", "x0")
SPREAD = ("core", "z2", "z1", "z0")
GATHER = ("core", "z2", "z1", "z0")
MERGE = ('y0', 'y1', 'y2')
LAST = ("x1", "x0")


def three_way(x):
    first = x.astype(BF16).astype(F32)
    rest = x - first
    second = rest.astype(BF16).astype(F32)
    return first, second, rest - second


def attend_kernel(
    fill_hbm, owner_hbm, q_hbm, k_hbm, v_hbm, nk_hbm, nv_hbm,
    ko_hbm, vo_hbm, out_ref,
    fill_ref, owner_ref, q_ref, nk_ref, nv_ref, k_ref, v_ref, q_rows, s_rows, rows_out, in_sem, load_sem, store_sem,
):
    steps, batch, width = q_ref.shape
    slots = k_ref.shape[1]
    heads = width // HD
    per_kv = heads // 2
    n = steps * heads
    size = batch // CHUNKS
    small = [
        pltpu.make_async_copy(src, dst, in_sem.at[i])
        for i, (src, dst) in enumerate(
            ((q_hbm, q_ref), (fill_hbm, fill_ref), (owner_hbm, owner_ref), (nk_hbm, nk_ref), (nv_hbm, nv_ref))
        )
    ]
    loads, stores = [[], []], [[], []]
    for i, (hbm, vmem, out) in enumerate(((k_hbm, k_ref, ko_hbm), (v_hbm, v_ref, vo_hbm))):
        for c in range(CHUNKS):
            part = pl.ds(c * size, size)
            loads[i].append(pltpu.make_async_copy(hbm.at[part], vmem.at[part], load_sem.at[i, c]))
            stores[i].append(pltpu.make_async_copy(vmem.at[part], out.at[part], store_sem.at[i, c]))
    for copy in small + loads[0] + loads[1]:
        copy.start()

    me = lax.axis_index(CTX)
    small[0].wait()
    q = q_ref[...].astype(F32)
    for s in range(steps):
        for h in range(heads):
            q_rows[:, s * heads + h, :] = q[s, :, h * HD : (h + 1) * HD]
    for copy in small[1:]:
        copy.wait()

    mine, ends = {}, {}
    for b in range(batch):
        end = fill_ref[0, b]
        for s in range(steps):
            mine[s, b] = owner_ref[s, b] == me
            end = end + mine[s, b].astype(jnp.int32)
            ends[s, b] = end

    def append(ref, new, b):
        for s in range(steps):

            @pl.when(mine[s, b])
            def _(s=s, slot=ends[s, b] - 1):
                base = pl.multiple_of((slot // 16) * 16, 16)
                at = lax.broadcasted_iota(jnp.int32, (16, 2 * HD), 0) == slot - base
                old = ref[b, pl.ds(base, 16), :].astype(F32)
                fresh = new[s, b : b + 1, :].astype(F32)
                ref[b, pl.ds(base, 16), :] = jnp.where(at, jnp.broadcast_to(fresh, at.shape), old).astype(BF16)

    row = lax.broadcasted_iota(jnp.int32, (n, slots), 0)
    slot_id = lax.broadcasted_iota(jnp.int32, (n, slots), 1)
    lane = lax.broadcasted_iota(jnp.int32, (heads, HD), 1)
    first = (lax.broadcasted_iota(jnp.int32, (n, HD), 0) // per_kv) % 2 == 0
    peaks = jnp.zeros((heads, HD), F32)
    totals = jnp.zeros((heads, HD), F32)
    gap = jnp.zeros((n, 2 * HD), BF16)
    rest = jnp.zeros((HD - 2 * n, 2 * HD), BF16)
    for c in range(CHUNKS):
        loads[0][c].wait()
        for b in range(c * size, (c + 1) * size):
            append(k_ref, nk_ref, b)
        stores[0][c].start()
    for pair in range(0, batch, 2):
        scores_t = jnp.zeros((slots, HD), F32)
        for b in (pair, pair + 1):
            q_b = q_rows[b]
            own = jnp.concatenate([jnp.where(first, q_b, 0.0), jnp.where(first, 0.0, q_b)], axis=1).astype(BF16)
            rhs = jnp.concatenate([own, gap, rest] if b == pair else [gap, own, rest], axis=0)
            scores_t = scores_t + lax.dot_general(
                k_ref[b], rhs, (((1,), (1,)), ((), ())), preferred_element_type=F32
            )
        s_rows[pair // 2] = scores_t.T
    for c in range(CHUNKS):
        loads[1][c].wait()
        for b in range(c * size, (c + 1) * size):
            append(v_ref, nv_ref, b)
        stores[1][c].start()
    for b in range(batch):
        length = jnp.where(row < heads, ends[0, b], ends[steps - 1, b])
        for s in range(1, steps - 1):
            length = jnp.where((row >= s * heads) & (row < (s + 1) * heads), ends[s, b], length)
        live = slot_id < length
        scores = s_rows[b // 2, (b % 2) * n : (b % 2 + 1) * n, :]
        masked = jnp.where(live, scores * (1.0 / HD**0.5), -1e30)
        peak = jnp.max(masked, axis=1, keepdims=True)
        weights = jnp.where(live, jnp.exp(masked - peak), 0.0)
        total = jnp.sum(weights, axis=1, keepdims=True)
        both = jnp.dot(weights.astype(BF16), v_ref[b], preferred_element_type=F32)
        part = jnp.where(first, both[:, :HD], both[:, HD:])
        for s in range(steps):
            own = slice(s * heads, (s + 1) * heads)
            at = s * batch + b
            rows_out[:, at, :] = part[own]
            peaks = jnp.where(lane == at, peak[own], peaks)
            totals = jnp.where(lane == at, total[own], totals)
    used = steps * batch
    for i, piece in enumerate(three_way(peaks) + three_way(totals)):
        rows_out[:, used + i, :] = piece
    for i in range(6, 8):
        rows_out[:, used + i, :] = jnp.zeros((heads, HD), F32)
    for h in range(heads):
        out_ref[h] = rows_out[h].astype(BF16)
    for copy in stores[0] + stores[1]:
        copy.wait()


def combined(in_ref):
    x = in_ref[...].astype(F32)
    used = x.shape[1] - 8
    stat = x[:, used:]
    row = lax.broadcasted_iota(jnp.int32, stat.shape, 1)
    peak = jnp.sum(jnp.where(row < 3, stat, 0.0), axis=1, keepdims=True)
    total = jnp.sum(jnp.where((row >= 3) & (row < 6), stat, 0.0), axis=1, keepdims=True)
    top = jnp.max(peak, axis=0, keepdims=True)
    factor = jnp.exp(peak - top)
    return x[:, :used], factor, top[0], jnp.sum(total * factor, axis=0)


def weighted(parts, factor):
    sources, rows, lanes = parts.shape
    shape = (1, rows, lanes)
    diagonal = lax.broadcasted_iota(jnp.int32, shape, 1) == lax.broadcasted_iota(jnp.int32, shape, 2)
    column = jnp.sum(jnp.where(diagonal, factor, 0.0), axis=2, keepdims=True)
    return jnp.sum(parts * column, axis=0)


def partial_kernel(in_ref, out_ref):
    parts, factor, top, total = combined(in_ref)
    row = lax.broadcasted_iota(jnp.int32, (8, HD), 0)
    stat = jnp.zeros((8, HD), F32)
    for i, piece in enumerate(three_way(top) + three_way(total)):
        stat = jnp.where(row == i, jnp.broadcast_to(piece, stat.shape), stat)
    block = jnp.concatenate([weighted(parts, factor), stat], axis=0).astype(BF16)
    for d in range(out_ref.shape[0]):
        out_ref[d] = block


def final_kernel(in_ref, out_ref):
    parts, factor, _, total = combined(in_ref)
    used = lax.broadcasted_iota(jnp.int32, total.shape, 1) < parts.shape[1]
    block = weighted(parts, factor / jnp.where(used, total, 1.0)[None]).astype(BF16)
    for d in range(out_ref.shape[0]):
        out_ref[d] = block


def place(index, order, wanted):
    bits = {axis: index >> (len(order) - 1 - i) & 1 for i, axis in enumerate(order)}
    return sum(bits[axis] << (len(wanted) - 1 - i) for i, axis in enumerate(wanted))


def project_kernel(in_ref, w_ref, out_ref):
    dests, batch, lanes = out_ref.shape
    steps = in_ref.shape[1] // batch
    each = w_ref.shape[0] // dests
    wide = jnp.concatenate([in_ref[place(h, SPREAD, GATHER)] for h in range(in_ref.shape[0])], axis=1)
    mixed = lax.dot_general(wide, w_ref[...], (((1,), (1,)), ((), ())), preferred_element_type=F32)
    rest = jnp.zeros((batch, lanes - steps * each), F32)
    for d in range(dests):
        pieces = [mixed[s * batch : (s + 1) * batch, d * each : (d + 1) * each] for s in range(steps)]
        out_ref[place(d, HEAD, LAST)] = jnp.concatenate(pieces + [rest], axis=1)


def finish_kernel(in_ref, out_ref):
    steps, batch, cols = out_ref.shape
    total = in_ref[0]
    for d in range(1, in_ref.shape[0]):
        total = total + in_ref[d]
    for s in range(steps):
        out_ref[s] = total[:, s * cols : (s + 1) * cols].astype(BF16)


VMEM = pl.BlockSpec(memory_space=pltpu.VMEM)
SMEM = pl.BlockSpec(memory_space=pltpu.SMEM)
HBM = pl.BlockSpec(memory_space=pltpu.HBM)


def on_device(n_y, n_zc, n_head, queries, k_cache, v_cache, new_keys, new_values, fill, owner, out_weight):
    steps, batch, width = queries.shape
    heads = width // HD
    used = steps * batch
    struct = jax.ShapeDtypeStruct
    params = lambda mib: pltpu.CompilerParams(vmem_limit_bytes=mib * 2**20)
    keys_out, values_out, sent = pl.pallas_call(
        attend_kernel,
        out_shape=(
            struct(k_cache.shape, BF16),
            struct(v_cache.shape, BF16),
            struct((n_zc, used + 8, HD), BF16),
        ),
        in_specs=[HBM] * 7,
        out_specs=(HBM, HBM, VMEM),
        scratch_shapes=[
            pltpu.SMEM((1, batch), jnp.int32),
            pltpu.SMEM(owner.shape, jnp.int32),
            pltpu.VMEM(queries.shape, BF16),
            pltpu.VMEM(new_keys.shape, BF16),
            pltpu.VMEM(new_values.shape, BF16),
            pltpu.VMEM(k_cache.shape, BF16),
            pltpu.VMEM(v_cache.shape, BF16),
            pltpu.VMEM((batch, steps * heads, HD), F32),
            pltpu.VMEM((batch // 2, HD, k_cache.shape[1]), F32),
            pltpu.VMEM((heads, used + 8, HD), F32),
            pltpu.SemaphoreType.DMA((5,)),
            pltpu.SemaphoreType.DMA((2, CHUNKS)),
            pltpu.SemaphoreType.DMA((2, CHUNKS)),
        ],
        compiler_params=pltpu.CompilerParams(vmem_limit_bytes=ATTEND_VMEM),
        name="attend",
    )(fill.T, owner, queries, k_cache, v_cache, new_keys, new_values)
    got = lax.all_to_all(sent, SPREAD, 0, 0)
    sent = pl.pallas_call(
        partial_kernel,
        out_shape=struct((n_y, used + 8, HD), BF16),
        in_specs=[VMEM],
        out_specs=VMEM,
        compiler_params=params(8),
        name="combine_zc",
    )(got)
    got = lax.all_to_all(sent, MERGE, 0, 0)
    sent = pl.pallas_call(
        final_kernel,
        out_shape=struct((n_zc, used, HD), BF16),
        in_specs=[VMEM],
        out_specs=VMEM,
        compiler_params=params(8),
        name="combine_y",
    )(got)
    got = lax.all_to_all(sent, GATHER, 0, 0)
    sent = pl.pallas_call(
        project_kernel,
        out_shape=struct((n_head, batch, 128), F32),
        in_specs=[VMEM, VMEM],
        out_specs=VMEM,
        compiler_params=params(8),
        name="project",
    )(got, out_weight.T)
    got = lax.all_to_all(sent, LAST, 0, 0)
    mixed = pl.pallas_call(
        finish_kernel,
        out_shape=struct((steps, batch, out_weight.shape[1] // n_head), BF16),
        in_specs=[VMEM],
        out_specs=VMEM,
        compiler_params=params(8),
        name="finish",
    )(got)
    return keys_out, values_out, mixed


def solution(mesh):
    split = Mesh(mesh.devices.reshape((2,) * 9), CTX + HEAD)
    in_specs = (
        P(None, None, HEAD),
        P(None, CTX, HEAD),
        P(None, CTX, HEAD),
        P(None, None, HEAD),
        P(None, None, HEAD),
        P(None, CTX),
        P(),
        P(HEAD, CTX),
    )
    out_specs = (P(None, CTX, HEAD), P(None, CTX, HEAD), P(None, None, CTX + HEAD))
    return jax.shard_map(
        functools.partial(on_device, 2 ** len(MERGE), 2 ** len(SPREAD), 2 ** len(HEAD)),
        mesh=split, in_specs=in_specs, out_specs=out_specs, check_vma=False,
    )
```

```python
import functools

import jax
import jax.numpy as jnp
from jax import lax
from jax.experimental import pallas as pl
from jax.experimental.pallas import tpu as pltpu
from jax.sharding import Mesh
from jax.sharding import PartitionSpec as P

HD = 128
F32 = jnp.float32
BF16 = jnp.bfloat16
ATTEND_VMEM = 63_000_000
CHUNKS = 1
CTX = ("y2", "y1", "y0", "z2", "z1", "z0", "core")
HEAD = ("x1", "x0")
SPREAD = ("core", "z2", "z1", "z0")
GATHER = ("core", "z2", "z1", "z0")
MERGE = ('y0', 'y1', 'y2')
LAST = ("x1", "x0")


def three_way(x):
    first = x.astype(BF16).astype(F32)
    rest = x - first
    second = rest.astype(BF16).astype(F32)
    return first, second, rest - second


def attend_kernel(
    fill_hbm, owner_hbm, q_hbm, k_hbm, v_hbm, nk_hbm, nv_hbm,
    ko_hbm, vo_hbm, out_hbm,
    fill_ref, owner_ref, q_ref, nk_ref, nv_ref, k_ref, v_ref, q_rows, s_rows, rows_out, out_ref, in_sem, load_sem, store_sem, out_sem,
):
    steps, batch, width = q_ref.shape
    slots = k_ref.shape[1]
    heads = width // HD
    per_kv = heads // 2
    n = steps * heads
    size = batch // CHUNKS
    small = [
        pltpu.make_async_copy(src, dst, in_sem.at[i])
        for i, (src, dst) in enumerate(
            ((q_hbm, q_ref), (fill_hbm, fill_ref), (owner_hbm, owner_ref), (nk_hbm, nk_ref), (nv_hbm, nv_ref))
        )
    ]
    loads, stores = [[], []], [[], []]
    for i, (hbm, vmem, out) in enumerate(((k_hbm, k_ref, ko_hbm), (v_hbm, v_ref, vo_hbm))):
        for c in range(CHUNKS):
            part = pl.ds(c * size, size)
            loads[i].append(pltpu.make_async_copy(hbm.at[part], vmem.at[part], load_sem.at[i, c]))
            stores[i].append(pltpu.make_async_copy(vmem.at[part], out.at[part], store_sem.at[i, c]))
    for copy in small + loads[0] + loads[1]:
        copy.start()

    me = lax.axis_index(CTX)
    small[0].wait()
    q = q_ref[...].astype(F32)
    for s in range(steps):
        for h in range(heads):
            q_rows[:, s * heads + h, :] = q[s, :, h * HD : (h + 1) * HD]
    for copy in small[1:]:
        copy.wait()

    mine, ends = {}, {}
    for b in range(batch):
        end = fill_ref[0, b]
        for s in range(steps):
            mine[s, b] = owner_ref[s, b] == me
            end = end + mine[s, b].astype(jnp.int32)
            ends[s, b] = end

    def append(ref, new, b):
        for s in range(steps):

            @pl.when(mine[s, b])
            def _(s=s, slot=ends[s, b] - 1):
                base = pl.multiple_of((slot // 16) * 16, 16)
                at = lax.broadcasted_iota(jnp.int32, (16, 2 * HD), 0) == slot - base
                old = ref[b, pl.ds(base, 16), :].astype(F32)
                fresh = new[s, b : b + 1, :].astype(F32)
                ref[b, pl.ds(base, 16), :] = jnp.where(at, jnp.broadcast_to(fresh, at.shape), old).astype(BF16)

    row = lax.broadcasted_iota(jnp.int32, (n, slots), 0)
    slot_id = lax.broadcasted_iota(jnp.int32, (n, slots), 1)
    lane = lax.broadcasted_iota(jnp.int32, (heads, HD), 1)
    first = (lax.broadcasted_iota(jnp.int32, (n, HD), 0) // per_kv) % 2 == 0
    peaks = jnp.zeros((heads, HD), F32)
    totals = jnp.zeros((heads, HD), F32)
    gap = jnp.zeros((n, 2 * HD), BF16)
    rest = jnp.zeros((HD - 2 * n, 2 * HD), BF16)
    for c in range(CHUNKS):
        loads[0][c].wait()
        for b in range(c * size, (c + 1) * size):
            append(k_ref, nk_ref, b)
        stores[0][c].start()
    for pair in range(0, batch, 2):
        scores_t = jnp.zeros((slots, HD), F32)
        for b in (pair, pair + 1):
            q_b = q_rows[b]
            own = jnp.concatenate([jnp.where(first, q_b, 0.0), jnp.where(first, 0.0, q_b)], axis=1).astype(BF16)
            rhs = jnp.concatenate([own, gap, rest] if b == pair else [gap, own, rest], axis=0)
            scores_t = scores_t + lax.dot_general(
                k_ref[b], rhs, (((1,), (1,)), ((), ())), preferred_element_type=F32
            )
        s_rows[pair // 2] = scores_t.T
    for c in range(CHUNKS):
        loads[1][c].wait()
        for b in range(c * size, (c + 1) * size):
            append(v_ref, nv_ref, b)
        stores[1][c].start()
    for b in range(batch):
        length = jnp.where(row < heads, ends[0, b], ends[steps - 1, b])
        for s in range(1, steps - 1):
            length = jnp.where((row >= s * heads) & (row < (s + 1) * heads), ends[s, b], length)
        live = slot_id < length
        scores = s_rows[b // 2, (b % 2) * n : (b % 2 + 1) * n, :]
        masked = jnp.where(live, scores * (1.0 / HD**0.5), -1e30)
        peak = jnp.max(masked, axis=1, keepdims=True)
        weights = jnp.where(live, jnp.exp(masked - peak), 0.0)
        total = jnp.sum(weights, axis=1, keepdims=True)
        both = jnp.dot(weights.astype(BF16), v_ref[b], preferred_element_type=F32)
        part = jnp.where(first, both[:, :HD], both[:, HD:])
        for s in range(steps):
            own = slice(s * heads, (s + 1) * heads)
            at = s * batch + b
            rows_out[:, at, :] = part[own]
            peaks = jnp.where(lane == at, peak[own], peaks)
            totals = jnp.where(lane == at, total[own], totals)
    used = steps * batch
    for i, piece in enumerate(three_way(peaks) + three_way(totals)):
        rows_out[:, used + i, :] = piece
    for i in range(6, 8):
        rows_out[:, used + i, :] = jnp.zeros((heads, HD), F32)
    for h in range(heads):
        out_ref[h] = rows_out[h].astype(BF16)
    sent = pltpu.make_async_copy(out_ref, out_hbm, out_sem)
    sent.start()
    for copy in stores[0] + stores[1] + [sent]:
        copy.wait()


def combined(in_ref):
    x = in_ref[...].astype(F32)
    used = x.shape[1] - 8
    stat = x[:, used:]
    row = lax.broadcasted_iota(jnp.int32, stat.shape, 1)
    peak = jnp.sum(jnp.where(row < 3, stat, 0.0), axis=1, keepdims=True)
    total = jnp.sum(jnp.where((row >= 3) & (row < 6), stat, 0.0), axis=1, keepdims=True)
    top = jnp.max(peak, axis=0, keepdims=True)
    factor = jnp.exp(peak - top)
    return x[:, :used], factor, top[0], jnp.sum(total * factor, axis=0)


def weighted(parts, factor):
    sources, rows, lanes = parts.shape
    shape = (1, rows, lanes)
    diagonal = lax.broadcasted_iota(jnp.int32, shape, 1) == lax.broadcasted_iota(jnp.int32, shape, 2)
    column = jnp.sum(jnp.where(diagonal, factor, 0.0), axis=2, keepdims=True)
    return jnp.sum(parts * column, axis=0)


def partial_kernel(in_ref, out_ref):
    parts, factor, top, total = combined(in_ref)
    row = lax.broadcasted_iota(jnp.int32, (8, HD), 0)
    stat = jnp.zeros((8, HD), F32)
    for i, piece in enumerate(three_way(top) + three_way(total)):
        stat = jnp.where(row == i, jnp.broadcast_to(piece, stat.shape), stat)
    block = jnp.concatenate([weighted(parts, factor), stat], axis=0).astype(BF16)
    for d in range(out_ref.shape[0]):
        out_ref[d] = block


def final_kernel(in_ref, out_ref):
    parts, factor, _, total = combined(in_ref)
    used = lax.broadcasted_iota(jnp.int32, total.shape, 1) < parts.shape[1]
    block = weighted(parts, factor / jnp.where(used, total, 1.0)[None]).astype(BF16)
    for d in range(out_ref.shape[0]):
        out_ref[d] = block


def place(index, order, wanted):
    bits = {axis: index >> (len(order) - 1 - i) & 1 for i, axis in enumerate(order)}
    return sum(bits[axis] << (len(wanted) - 1 - i) for i, axis in enumerate(wanted))


def project_kernel(in_ref, w_ref, out_ref):
    dests, batch, lanes = out_ref.shape
    steps = in_ref.shape[1] // batch
    each = w_ref.shape[0] // dests
    wide = jnp.concatenate([in_ref[place(h, SPREAD, GATHER)] for h in range(in_ref.shape[0])], axis=1)
    mixed = lax.dot_general(wide, w_ref[...], (((1,), (1,)), ((), ())), preferred_element_type=F32)
    rest = jnp.zeros((batch, lanes - steps * each), F32)
    for d in range(dests):
        pieces = [mixed[s * batch : (s + 1) * batch, d * each : (d + 1) * each] for s in range(steps)]
        out_ref[place(d, HEAD, LAST)] = jnp.concatenate(pieces + [rest], axis=1)


def finish_kernel(in_ref, out_ref):
    steps, batch, cols = out_ref.shape
    total = in_ref[0]
    for d in range(1, in_ref.shape[0]):
        total = total + in_ref[d]
    for s in range(steps):
        out_ref[s] = total[:, s * cols : (s + 1) * cols].astype(BF16)


VMEM = pl.BlockSpec(memory_space=pltpu.VMEM)
SMEM = pl.BlockSpec(memory_space=pltpu.SMEM)
HBM = pl.BlockSpec(memory_space=pltpu.HBM)


def on_device(n_y, n_zc, n_head, queries, k_cache, v_cache, new_keys, new_values, fill, owner, out_weight):
    steps, batch, width = queries.shape
    heads = width // HD
    used = steps * batch
    struct = jax.ShapeDtypeStruct
    params = lambda mib: pltpu.CompilerParams(vmem_limit_bytes=mib * 2**20)
    keys_out, values_out, sent = pl.pallas_call(
        attend_kernel,
        out_shape=(
            struct(k_cache.shape, BF16),
            struct(v_cache.shape, BF16),
            struct((n_zc, used + 8, HD), BF16),
        ),
        in_specs=[HBM] * 7,
        out_specs=(HBM, HBM, HBM),
        scratch_shapes=[
            pltpu.SMEM((1, batch), jnp.int32),
            pltpu.SMEM(owner.shape, jnp.int32),
            pltpu.VMEM(queries.shape, BF16),
            pltpu.VMEM(new_keys.shape, BF16),
            pltpu.VMEM(new_values.shape, BF16),
            pltpu.VMEM(k_cache.shape, BF16),
            pltpu.VMEM(v_cache.shape, BF16),
            pltpu.VMEM((batch, steps * heads, HD), F32),
            pltpu.VMEM((batch // 2, HD, k_cache.shape[1]), F32),
            pltpu.VMEM((heads, used + 8, HD), F32),
            pltpu.VMEM((n_zc, used + 8, HD), BF16),
            pltpu.SemaphoreType.DMA((5,)),
            pltpu.SemaphoreType.DMA((2, CHUNKS)),
            pltpu.SemaphoreType.DMA((2, CHUNKS)),
            pltpu.SemaphoreType.DMA,
        ],
        compiler_params=pltpu.CompilerParams(vmem_limit_bytes=ATTEND_VMEM),
        name="attend",
    )(fill.T, owner, queries, k_cache, v_cache, new_keys, new_values)
    got = lax.all_to_all(sent, SPREAD, 0, 0)
    sent = pl.pallas_call(
        partial_kernel,
        out_shape=struct((n_y, used + 8, HD), BF16),
        in_specs=[VMEM],
        out_specs=VMEM,
        compiler_params=params(8),
        name="combine_zc",
    )(got)
    got = lax.all_to_all(sent, MERGE, 0, 0)
    sent = pl.pallas_call(
        final_kernel,
        out_shape=struct((n_zc, used, HD), BF16),
        in_specs=[VMEM],
        out_specs=VMEM,
        compiler_params=params(8),
        name="combine_y",
    )(got)
    got = lax.all_to_all(sent, GATHER, 0, 0)
    sent = pl.pallas_call(
        project_kernel,
        out_shape=struct((n_head, batch, 128), F32),
        in_specs=[VMEM, VMEM],
        out_specs=VMEM,
        compiler_params=params(8),
        name="project",
    )(got, out_weight.T)
    got = lax.all_to_all(sent, LAST, 0, 0)
    mixed = pl.pallas_call(
        finish_kernel,
        out_shape=struct((steps, batch, out_weight.shape[1] // n_head), BF16),
        in_specs=[VMEM],
        out_specs=VMEM,
        compiler_params=params(8),
        name="finish",
    )(got)
    return keys_out, values_out, mixed


def solution(mesh):
    split = Mesh(mesh.devices.reshape((2,) * 9), CTX + HEAD)
    in_specs = (
        P(None, None, HEAD),
        P(None, CTX, HEAD),
        P(None, CTX, HEAD),
        P(None, None, HEAD),
        P(None, None, HEAD),
        P(None, CTX),
        P(),
        P(HEAD, CTX),
    )
    out_specs = (P(None, CTX, HEAD), P(None, CTX, HEAD), P(None, None, CTX + HEAD))
    return jax.shard_map(
        functools.partial(on_device, 2 ** len(MERGE), 2 ** len(SPREAD), 2 ** len(HEAD)),
        mesh=split, in_specs=in_specs, out_specs=out_specs, check_vma=False,
    )
```

```python
import functools

import jax
import jax.numpy as jnp
from jax import lax
from jax.experimental import pallas as pl
from jax.experimental.pallas import tpu as pltpu
from jax.sharding import Mesh
from jax.sharding import PartitionSpec as P

HD = 128
F32 = jnp.float32
BF16 = jnp.bfloat16
ATTEND_VMEM = 63_000_000
CTX = ("y2", "y1", "y0", "z2", "z1", "z0", "core")
HEAD = ("x1", "x0")
SPREAD = ("core", "z2", "z1", "z0")
GATHER = ("core", "z2", "z1", "z0")
MERGE = ('y0', 'y1', 'y2')
LAST = ("x1", "x0")


def three_way(x):
    first = x.astype(BF16).astype(F32)
    rest = x - first
    second = rest.astype(BF16).astype(F32)
    return first, second, rest - second


def attend_kernel(
    fill_hbm, owner_hbm, q_hbm, k_hbm, v_hbm, nk_hbm, nv_hbm,
    ko_hbm, vo_hbm, out_hbm,
    fill_ref, owner_ref, q_ref, nk_ref, nv_ref, k_ref, v_ref, q_rows, s_rows, rows_out, out_ref, in_sem, load_sem, store_sem, out_sem,
):
    steps, batch, width = q_ref.shape
    slots = k_ref.shape[1]
    heads = width // HD
    per_kv = heads // 2
    n = steps * heads
    small = [
        pltpu.make_async_copy(src, dst, in_sem.at[i])
        for i, (src, dst) in enumerate(
            ((q_hbm, q_ref), (fill_hbm, fill_ref), (owner_hbm, owner_ref), (nk_hbm, nk_ref), (nv_hbm, nv_ref))
        )
    ]
    loads, stores = [], []
    for i, (hbm, vmem, out) in enumerate(((k_hbm, k_ref, ko_hbm), (v_hbm, v_ref, vo_hbm))):
        loads.append(pltpu.make_async_copy(hbm, vmem, load_sem.at[i]))
        stores.append(pltpu.make_async_copy(vmem, out, store_sem.at[i]))
    for copy in small + loads:
        copy.start()

    me = lax.axis_index(CTX)
    small[0].wait()
    q = q_ref[...].astype(F32)
    for s in range(steps):
        for h in range(heads):
            q_rows[:, s * heads + h, :] = q[s, :, h * HD : (h + 1) * HD]
    for copy in small[1:]:
        copy.wait()

    mine, ends = {}, {}
    for b in range(batch):
        end = fill_ref[0, b]
        for s in range(steps):
            mine[s, b] = owner_ref[s, b] == me
            end = end + mine[s, b].astype(jnp.int32)
            ends[s, b] = end

    def append(ref, new, b):
        for s in range(steps):

            @pl.when(mine[s, b])
            def _(s=s, slot=ends[s, b] - 1):
                base = pl.multiple_of((slot // 16) * 16, 16)
                at = lax.broadcasted_iota(jnp.int32, (16, 2 * HD), 0) == slot - base
                old = ref[b, pl.ds(base, 16), :].astype(F32)
                fresh = new[s, b : b + 1, :].astype(F32)
                ref[b, pl.ds(base, 16), :] = jnp.where(at, jnp.broadcast_to(fresh, at.shape), old).astype(BF16)

    row = lax.broadcasted_iota(jnp.int32, (n, slots), 0)
    slot_id = lax.broadcasted_iota(jnp.int32, (n, slots), 1)
    lane = lax.broadcasted_iota(jnp.int32, (heads, HD), 1)
    first = (lax.broadcasted_iota(jnp.int32, (n, HD), 0) // per_kv) % 2 == 0
    peaks = jnp.zeros((heads, HD), F32)
    totals = jnp.zeros((heads, HD), F32)
    gap = jnp.zeros((n, 2 * HD), BF16)
    rest = jnp.zeros((HD - 2 * n, 2 * HD), BF16)
    some = functools.reduce(jnp.logical_or, mine.values())
    loads[0].wait()

    @pl.when(some)
    def _():
        for b in range(batch):
            append(k_ref, nk_ref, b)

    stores[0].start()
    for pair in range(0, batch, 2):
        scores_t = jnp.zeros((slots, HD), F32)
        for b in (pair, pair + 1):
            q_b = q_rows[b]
            own = jnp.concatenate([jnp.where(first, q_b, 0.0), jnp.where(first, 0.0, q_b)], axis=1).astype(BF16)
            rhs = jnp.concatenate([own, gap, rest] if b == pair else [gap, own, rest], axis=0)
            scores_t = scores_t + lax.dot_general(
                k_ref[b], rhs, (((1,), (1,)), ((), ())), preferred_element_type=F32
            )
        s_rows[pair // 2] = scores_t.T
    loads[1].wait()

    @pl.when(some)
    def _():
        for b in range(batch):
            append(v_ref, nv_ref, b)

    stores[1].start()
    for b in range(batch):
        length = jnp.where(row < heads, ends[0, b], ends[steps - 1, b])
        for s in range(1, steps - 1):
            length = jnp.where((row >= s * heads) & (row < (s + 1) * heads), ends[s, b], length)
        live = slot_id < length
        scores = s_rows[b // 2, (b % 2) * n : (b % 2 + 1) * n, :]
        masked = jnp.where(live, scores * (1.0 / HD**0.5), -1e30)
        peak = jnp.max(masked, axis=1, keepdims=True)
        weights = jnp.where(live, jnp.exp(masked - peak), 0.0)
        total = jnp.sum(weights, axis=1, keepdims=True)
        both = jnp.dot(weights.astype(BF16), v_ref[b], preferred_element_type=F32)
        part = jnp.where(first, both[:, :HD], both[:, HD:])
        for s in range(steps):
            own = slice(s * heads, (s + 1) * heads)
            at = s * batch + b
            rows_out[:, at, :] = part[own]
            peaks = jnp.where(lane == at, peak[own], peaks)
            totals = jnp.where(lane == at, total[own], totals)
    used = steps * batch
    for i, piece in enumerate(three_way(peaks) + three_way(totals)):
        rows_out[:, used + i, :] = piece
    for i in range(6, 8):
        rows_out[:, used + i, :] = jnp.zeros((heads, HD), F32)
    for h in range(heads):
        out_ref[h] = rows_out[h].astype(BF16)
    sent = pltpu.make_async_copy(out_ref, out_hbm, out_sem)
    sent.start()
    for copy in stores + [sent]:
        copy.wait()


def combined(in_ref):
    x = in_ref[...].astype(F32)
    used = x.shape[1] - 8
    stat = x[:, used:]
    row = lax.broadcasted_iota(jnp.int32, stat.shape, 1)
    peak = jnp.sum(jnp.where(row < 3, stat, 0.0), axis=1, keepdims=True)
    total = jnp.sum(jnp.where((row >= 3) & (row < 6), stat, 0.0), axis=1, keepdims=True)
    top = jnp.max(peak, axis=0, keepdims=True)
    factor = jnp.exp(peak - top)
    return x[:, :used], factor, top[0], jnp.sum(total * factor, axis=0)


def weighted(parts, factor):
    sources, rows, lanes = parts.shape
    shape = (1, rows, lanes)
    diagonal = lax.broadcasted_iota(jnp.int32, shape, 1) == lax.broadcasted_iota(jnp.int32, shape, 2)
    column = jnp.sum(jnp.where(diagonal, factor, 0.0), axis=2, keepdims=True)
    return jnp.sum(parts * column, axis=0)


def partial_kernel(in_ref, out_ref):
    parts, factor, top, total = combined(in_ref)
    row = lax.broadcasted_iota(jnp.int32, (8, HD), 0)
    stat = jnp.zeros((8, HD), F32)
    for i, piece in enumerate(three_way(top) + three_way(total)):
        stat = jnp.where(row == i, jnp.broadcast_to(piece, stat.shape), stat)
    block = jnp.concatenate([weighted(parts, factor), stat], axis=0).astype(BF16)
    for d in range(out_ref.shape[0]):
        out_ref[d] = block


def final_kernel(in_ref, out_ref):
    parts, factor, _, total = combined(in_ref)
    used = lax.broadcasted_iota(jnp.int32, total.shape, 1) < parts.shape[1]
    block = weighted(parts, factor / jnp.where(used, total, 1.0)[None]).astype(BF16)
    for d in range(out_ref.shape[0]):
        out_ref[d] = block


def place(index, order, wanted):
    bits = {axis: index >> (len(order) - 1 - i) & 1 for i, axis in enumerate(order)}
    return sum(bits[axis] << (len(wanted) - 1 - i) for i, axis in enumerate(wanted))


def project_kernel(in_ref, w_ref, out_ref):
    dests, batch, lanes = out_ref.shape
    steps = in_ref.shape[1] // batch
    each = w_ref.shape[0] // dests
    wide = jnp.concatenate([in_ref[place(h, SPREAD, GATHER)] for h in range(in_ref.shape[0])], axis=1)
    mixed = lax.dot_general(wide, w_ref[...], (((1,), (1,)), ((), ())), preferred_element_type=F32)
    rest = jnp.zeros((batch, lanes - steps * each), F32)
    for d in range(dests):
        pieces = [mixed[s * batch : (s + 1) * batch, d * each : (d + 1) * each] for s in range(steps)]
        out_ref[place(d, HEAD, LAST)] = jnp.concatenate(pieces + [rest], axis=1)


def finish_kernel(in_ref, out_ref):
    steps, batch, cols = out_ref.shape
    total = in_ref[0]
    for d in range(1, in_ref.shape[0]):
        total = total + in_ref[d]
    for s in range(steps):
        out_ref[s] = total[:, s * cols : (s + 1) * cols].astype(BF16)


VMEM = pl.BlockSpec(memory_space=pltpu.VMEM)
SMEM = pl.BlockSpec(memory_space=pltpu.SMEM)
HBM = pl.BlockSpec(memory_space=pltpu.HBM)


def on_device(n_y, n_zc, n_head, queries, k_cache, v_cache, new_keys, new_values, fill, owner, out_weight):
    steps, batch, width = queries.shape
    heads = width // HD
    used = steps * batch
    struct = jax.ShapeDtypeStruct
    params = lambda mib: pltpu.CompilerParams(vmem_limit_bytes=mib * 2**20)
    keys_out, values_out, sent = pl.pallas_call(
        attend_kernel,
        out_shape=(
            struct(k_cache.shape, BF16),
            struct(v_cache.shape, BF16),
            struct((n_zc, used + 8, HD), BF16),
        ),
        in_specs=[HBM] * 7,
        out_specs=(HBM, HBM, HBM),
        scratch_shapes=[
            pltpu.SMEM((1, batch), jnp.int32),
            pltpu.SMEM(owner.shape, jnp.int32),
            pltpu.VMEM(queries.shape, BF16),
            pltpu.VMEM(new_keys.shape, BF16),
            pltpu.VMEM(new_values.shape, BF16),
            pltpu.VMEM(k_cache.shape, BF16),
            pltpu.VMEM(v_cache.shape, BF16),
            pltpu.VMEM((batch, steps * heads, HD), F32),
            pltpu.VMEM((batch // 2, HD, k_cache.shape[1]), F32),
            pltpu.VMEM((heads, used + 8, HD), F32),
            pltpu.VMEM((n_zc, used + 8, HD), BF16),
            pltpu.SemaphoreType.DMA((5,)),
            pltpu.SemaphoreType.DMA((2,)),
            pltpu.SemaphoreType.DMA((2,)),
            pltpu.SemaphoreType.DMA,
        ],
        compiler_params=pltpu.CompilerParams(vmem_limit_bytes=ATTEND_VMEM),
        name="attend",
    )(fill.T, owner, queries, k_cache, v_cache, new_keys, new_values)
    got = lax.all_to_all(sent, SPREAD, 0, 0)
    sent = pl.pallas_call(
        partial_kernel,
        out_shape=struct((n_y, used + 8, HD), BF16),
        in_specs=[VMEM],
        out_specs=VMEM,
        compiler_params=params(8),
        name="combine_zc",
    )(got)
    got = lax.all_to_all(sent, MERGE, 0, 0)
    sent = pl.pallas_call(
        final_kernel,
        out_shape=struct((n_zc, used, HD), BF16),
        in_specs=[VMEM],
        out_specs=VMEM,
        compiler_params=params(8),
        name="combine_y",
    )(got)
    got = lax.all_to_all(sent, GATHER, 0, 0)
    sent = pl.pallas_call(
        project_kernel,
        out_shape=struct((n_head, batch, 128), F32),
        in_specs=[VMEM, VMEM],
        out_specs=VMEM,
        compiler_params=params(8),
        name="project",
    )(got, out_weight.T)
    got = lax.all_to_all(sent, LAST, 0, 0)
    mixed = pl.pallas_call(
        finish_kernel,
        out_shape=struct((steps, batch, out_weight.shape[1] // n_head), BF16),
        in_specs=[VMEM],
        out_specs=VMEM,
        compiler_params=params(8),
        name="finish",
    )(got)
    return keys_out, values_out, mixed


def solution(mesh):
    split = Mesh(mesh.devices.reshape((2,) * 9), CTX + HEAD)
    in_specs = (
        P(None, None, HEAD),
        P(None, CTX, HEAD),
        P(None, CTX, HEAD),
        P(None, None, HEAD),
        P(None, None, HEAD),
        P(None, CTX),
        P(),
        P(HEAD, CTX),
    )
    out_specs = (P(None, CTX, HEAD), P(None, CTX, HEAD), P(None, None, CTX + HEAD))
    return jax.shard_map(
        functools.partial(on_device, 2 ** len(MERGE), 2 ** len(SPREAD), 2 ** len(HEAD)),
        mesh=split, in_specs=in_specs, out_specs=out_specs, check_vma=False,
    )
```

```python
import functools

import jax
import jax.numpy as jnp
from jax import lax
from jax.experimental import pallas as pl
from jax.experimental.pallas import tpu as pltpu
from jax.sharding import Mesh
from jax.sharding import PartitionSpec as P

HD = 128
F32 = jnp.float32
BF16 = jnp.bfloat16
ATTEND_VMEM = 63_000_000
CTX = ("y2", "y1", "y0", "z2", "z1", "z0", "core")
HEAD = ("x1", "x0")
SPREAD = ("core", "z1", "z2", "z0")
GATHER = ("core", "z1", "z2", "z0")
MERGE = ('y0', 'y1', 'y2')
LAST = ("x1", "x0")


def three_way(x):
    first = x.astype(BF16).astype(F32)
    rest = x - first
    second = rest.astype(BF16).astype(F32)
    return first, second, rest - second


def attend_kernel(
    fill_hbm, owner_hbm, q_hbm, k_hbm, v_hbm, nk_hbm, nv_hbm,
    ko_hbm, vo_hbm, out_hbm,
    fill_ref, owner_ref, q_ref, nk_ref, nv_ref, k_ref, v_ref, q_rows, s_rows, rows_out, out_ref, in_sem, load_sem, store_sem, out_sem,
):
    steps, batch, width = q_ref.shape
    slots = k_ref.shape[1]
    heads = width // HD
    per_kv = heads // 2
    n = steps * heads
    small = [
        pltpu.make_async_copy(src, dst, in_sem.at[i])
        for i, (src, dst) in enumerate(
            ((q_hbm, q_ref), (fill_hbm, fill_ref), (owner_hbm, owner_ref), (nk_hbm, nk_ref), (nv_hbm, nv_ref))
        )
    ]
    loads, stores = [], []
    for i, (hbm, vmem, out) in enumerate(((k_hbm, k_ref, ko_hbm), (v_hbm, v_ref, vo_hbm))):
        loads.append(pltpu.make_async_copy(hbm, vmem, load_sem.at[i]))
        stores.append(pltpu.make_async_copy(vmem, out, store_sem.at[i]))
    for copy in small + loads:
        copy.start()

    me = lax.axis_index(CTX)
    small[0].wait()
    q = q_ref[...].astype(F32)
    for s in range(steps):
        for h in range(heads):
            q_rows[:, s * heads + h, :] = q[s, :, h * HD : (h + 1) * HD]
    for copy in small[1:]:
        copy.wait()

    mine, ends = {}, {}
    for b in range(batch):
        end = fill_ref[0, b]
        for s in range(steps):
            mine[s, b] = owner_ref[s, b] == me
            end = end + mine[s, b].astype(jnp.int32)
            ends[s, b] = end

    def append(ref, new, b):
        for s in range(steps):

            @pl.when(mine[s, b])
            def _(s=s, slot=ends[s, b] - 1):
                base = pl.multiple_of((slot // 16) * 16, 16)
                at = lax.broadcasted_iota(jnp.int32, (16, 2 * HD), 0) == slot - base
                old = ref[b, pl.ds(base, 16), :].astype(F32)
                fresh = new[s, b : b + 1, :].astype(F32)
                ref[b, pl.ds(base, 16), :] = jnp.where(at, jnp.broadcast_to(fresh, at.shape), old).astype(BF16)

    row = lax.broadcasted_iota(jnp.int32, (n, slots), 0)
    slot_id = lax.broadcasted_iota(jnp.int32, (n, slots), 1)
    lane = lax.broadcasted_iota(jnp.int32, (heads, HD), 1)
    first = (lax.broadcasted_iota(jnp.int32, (n, HD), 0) // per_kv) % 2 == 0
    peaks = jnp.zeros((heads, HD), F32)
    totals = jnp.zeros((heads, HD), F32)
    gap = jnp.zeros((n, 2 * HD), BF16)
    rest = jnp.zeros((HD - 2 * n, 2 * HD), BF16)
    some = functools.reduce(jnp.logical_or, mine.values())
    loads[0].wait()

    @pl.when(some)
    def _():
        for b in range(batch):
            append(k_ref, nk_ref, b)

    stores[0].start()
    for pair in range(0, batch, 2):
        scores_t = jnp.zeros((slots, HD), F32)
        for b in (pair, pair + 1):
            q_b = q_rows[b]
            own = jnp.concatenate([jnp.where(first, q_b, 0.0), jnp.where(first, 0.0, q_b)], axis=1).astype(BF16)
            rhs = jnp.concatenate([own, gap, rest] if b == pair else [gap, own, rest], axis=0)
            scores_t = scores_t + lax.dot_general(
                k_ref[b], rhs, (((1,), (1,)), ((), ())), preferred_element_type=F32
            )
        s_rows[pair // 2] = scores_t.T
    loads[1].wait()

    @pl.when(some)
    def _():
        for b in range(batch):
            append(v_ref, nv_ref, b)

    stores[1].start()
    for b in range(batch):
        length = jnp.where(row < heads, ends[0, b], ends[steps - 1, b])
        for s in range(1, steps - 1):
            length = jnp.where((row >= s * heads) & (row < (s + 1) * heads), ends[s, b], length)
        live = slot_id < length
        scores = s_rows[b // 2, (b % 2) * n : (b % 2 + 1) * n, :]
        masked = jnp.where(live, scores * (1.0 / HD**0.5), -1e30)
        peak = jnp.max(masked, axis=1, keepdims=True)
        weights = jnp.where(live, jnp.exp(masked - peak), 0.0)
        total = jnp.sum(weights, axis=1, keepdims=True)
        both = jnp.dot(weights.astype(BF16), v_ref[b], preferred_element_type=F32)
        part = jnp.where(first, both[:, :HD], both[:, HD:])
        for s in range(steps):
            own = slice(s * heads, (s + 1) * heads)
            at = s * batch + b
            rows_out[:, at, :] = part[own]
            peaks = jnp.where(lane == at, peak[own], peaks)
            totals = jnp.where(lane == at, total[own], totals)
    used = steps * batch
    for i, piece in enumerate(three_way(peaks) + three_way(totals)):
        rows_out[:, used + i, :] = piece
    for i in range(6, 8):
        rows_out[:, used + i, :] = jnp.zeros((heads, HD), F32)
    for h in range(heads):
        out_ref[h] = rows_out[h].astype(BF16)
    sent = pltpu.make_async_copy(out_ref, out_hbm, out_sem)
    sent.start()
    for copy in stores + [sent]:
        copy.wait()


def combined(in_ref):
    x = in_ref[...].astype(F32)
    used = x.shape[1] - 8
    stat = x[:, used:]
    row = lax.broadcasted_iota(jnp.int32, stat.shape, 1)
    peak = jnp.sum(jnp.where(row < 3, stat, 0.0), axis=1, keepdims=True)
    total = jnp.sum(jnp.where((row >= 3) & (row < 6), stat, 0.0), axis=1, keepdims=True)
    top = jnp.max(peak, axis=0, keepdims=True)
    factor = jnp.exp(peak - top)
    return x[:, :used], factor, top[0], jnp.sum(total * factor, axis=0)


def weighted(parts, factor):
    sources, rows, lanes = parts.shape
    shape = (1, rows, lanes)
    diagonal = lax.broadcasted_iota(jnp.int32, shape, 1) == lax.broadcasted_iota(jnp.int32, shape, 2)
    column = jnp.sum(jnp.where(diagonal, factor, 0.0), axis=2, keepdims=True)
    return jnp.sum(parts * column, axis=0)


def partial_kernel(in_ref, out_ref):
    parts, factor, top, total = combined(in_ref)
    row = lax.broadcasted_iota(jnp.int32, (8, HD), 0)
    stat = jnp.zeros((8, HD), F32)
    for i, piece in enumerate(three_way(top) + three_way(total)):
        stat = jnp.where(row == i, jnp.broadcast_to(piece, stat.shape), stat)
    block = jnp.concatenate([weighted(parts, factor), stat], axis=0).astype(BF16)
    for d in range(out_ref.shape[0]):
        out_ref[d] = block


def final_kernel(in_ref, out_ref):
    parts, factor, _, total = combined(in_ref)
    used = lax.broadcasted_iota(jnp.int32, total.shape, 1) < parts.shape[1]
    block = weighted(parts, factor / jnp.where(used, total, 1.0)[None]).astype(BF16)
    for d in range(out_ref.shape[0]):
        out_ref[d] = block


def place(index, order, wanted):
    bits = {axis: index >> (len(order) - 1 - i) & 1 for i, axis in enumerate(order)}
    return sum(bits[axis] << (len(wanted) - 1 - i) for i, axis in enumerate(wanted))


def project_kernel(in_ref, w_ref, out_ref):
    dests, batch, lanes = out_ref.shape
    steps = in_ref.shape[1] // batch
    each = w_ref.shape[0] // dests
    wide = jnp.concatenate([in_ref[place(h, SPREAD, GATHER)] for h in range(in_ref.shape[0])], axis=1)
    mixed = lax.dot_general(wide, w_ref[...], (((1,), (1,)), ((), ())), preferred_element_type=F32)
    rest = jnp.zeros((batch, lanes - steps * each), F32)
    for d in range(dests):
        pieces = [mixed[s * batch : (s + 1) * batch, d * each : (d + 1) * each] for s in range(steps)]
        out_ref[place(d, HEAD, LAST)] = jnp.concatenate(pieces + [rest], axis=1)


def finish_kernel(in_ref, out_ref):
    steps, batch, cols = out_ref.shape
    total = in_ref[0]
    for d in range(1, in_ref.shape[0]):
        total = total + in_ref[d]
    for s in range(steps):
        out_ref[s] = total[:, s * cols : (s + 1) * cols].astype(BF16)


VMEM = pl.BlockSpec(memory_space=pltpu.VMEM)
SMEM = pl.BlockSpec(memory_space=pltpu.SMEM)
HBM = pl.BlockSpec(memory_space=pltpu.HBM)


def on_device(n_y, n_zc, n_head, queries, k_cache, v_cache, new_keys, new_values, fill, owner, out_weight):
    steps, batch, width = queries.shape
    heads = width // HD
    used = steps * batch
    struct = jax.ShapeDtypeStruct
    params = lambda mib: pltpu.CompilerParams(vmem_limit_bytes=mib * 2**20)
    keys_out, values_out, sent = pl.pallas_call(
        attend_kernel,
        out_shape=(
            struct(k_cache.shape, BF16),
            struct(v_cache.shape, BF16),
            struct((n_zc, used + 8, HD), BF16),
        ),
        in_specs=[HBM] * 7,
        out_specs=(HBM, HBM, HBM),
        scratch_shapes=[
            pltpu.SMEM((1, batch), jnp.int32),
            pltpu.SMEM(owner.shape, jnp.int32),
            pltpu.VMEM(queries.shape, BF16),
            pltpu.VMEM(new_keys.shape, BF16),
            pltpu.VMEM(new_values.shape, BF16),
            pltpu.VMEM(k_cache.shape, BF16),
            pltpu.VMEM(v_cache.shape, BF16),
            pltpu.VMEM((batch, steps * heads, HD), F32),
            pltpu.VMEM((batch // 2, HD, k_cache.shape[1]), F32),
            pltpu.VMEM((heads, used + 8, HD), F32),
            pltpu.VMEM((n_zc, used + 8, HD), BF16),
            pltpu.SemaphoreType.DMA((5,)),
            pltpu.SemaphoreType.DMA((2,)),
            pltpu.SemaphoreType.DMA((2,)),
            pltpu.SemaphoreType.DMA,
        ],
        compiler_params=pltpu.CompilerParams(vmem_limit_bytes=ATTEND_VMEM),
        name="attend",
    )(fill.T, owner, queries, k_cache, v_cache, new_keys, new_values)
    got = lax.all_to_all(sent, SPREAD, 0, 0)
    sent = pl.pallas_call(
        partial_kernel,
        out_shape=struct((n_y, used + 8, HD), BF16),
        in_specs=[VMEM],
        out_specs=VMEM,
        compiler_params=params(8),
        name="combine_zc",
    )(got)
    got = lax.all_to_all(sent, MERGE, 0, 0)
    sent = pl.pallas_call(
        final_kernel,
        out_shape=struct((n_zc, used, HD), BF16),
        in_specs=[VMEM],
        out_specs=VMEM,
        compiler_params=params(8),
        name="combine_y",
    )(got)
    got = lax.all_to_all(sent, GATHER, 0, 0)
    sent = pl.pallas_call(
        project_kernel,
        out_shape=struct((n_head, batch, 128), F32),
        in_specs=[VMEM, VMEM],
        out_specs=VMEM,
        compiler_params=params(8),
        name="project",
    )(got, out_weight.T)
    got = lax.all_to_all(sent, LAST, 0, 0)
    mixed = pl.pallas_call(
        finish_kernel,
        out_shape=struct((steps, batch, out_weight.shape[1] // n_head), BF16),
        in_specs=[VMEM],
        out_specs=VMEM,
        compiler_params=params(8),
        name="finish",
    )(got)
    return keys_out, values_out, mixed


def solution(mesh):
    split = Mesh(mesh.devices.reshape((2,) * 9), CTX + HEAD)
    in_specs = (
        P(None, None, HEAD),
        P(None, CTX, HEAD),
        P(None, CTX, HEAD),
        P(None, None, HEAD),
        P(None, None, HEAD),
        P(None, CTX),
        P(),
        P(HEAD, CTX),
    )
    out_specs = (P(None, CTX, HEAD), P(None, CTX, HEAD), P(None, None, CTX + HEAD))
    return jax.shard_map(
        functools.partial(on_device, 2 ** len(MERGE), 2 ** len(SPREAD), 2 ** len(HEAD)),
        mesh=split, in_specs=in_specs, out_specs=out_specs, check_vma=False,
    )
```
